32 devices in a mesh: grp: 8 (over z, x), own: 4 (over y, core).
Axes of the slice: x: 2, y: 2, z: 4, core: 2. Of those that a mesh axis runs over, the one named last changes fastest.
Arguments:
- queries: bfloat16 [2048, 768], P(('grp', 'own')), may hold values from -6 to 6
- projection: bfloat16 [768, 768], replicated, may hold values from -0.21875 to 0.21875
- lists: bfloat16 [1024, 256, 768], P(('grp', 'own')), may hold values from -6 to 6
- probes: int32 [2048, 8], P(('grp', 'own')), may hold values from 0 to 1023, as said below
- owner_map: int32 [1024], replicated, may hold values from 0 to 1023, as said below
Outputs:
- scores: float32 [2048, 8, 256], P(('grp', 'own'))
The draws below stay inside these ranges and needn't reach their ends.
Inputs may be any that keep to these rules, and one draw needn't show every extreme that they name: A permutation: list i is stored in slot owner_map[i], slots k * 32 to (k + 1) * 32 - 1 lying on the k-th device of grp+own. `probes`: a query's 8 list ids are distinct; the 64 queries of one device probe lists stored on any one device at most 32 times in all; all queries together probe any one stored list at most 32 times.
All inputs are finite; a program needn't handle non-finite values.
Results may differ from the reference program's by a relative error of at most 0.0003.
Values may be sent and summed in bfloat16 or wider, within the bound.
A program may use at most 64 MiB of HBM per device.

```python
import jax
import jax.numpy as jnp
from jax import lax

D = 768
LSIZE = 256
NPROBE = 8
LISTS_DEV = 32
Q_DEV = 64
NLIST = 1024
NQ = 2048


def probe_plan(key):
    device_count = NLIST // LISTS_DEV
    pair_count = Q_DEV * NPROBE
    mean_load = pair_count // device_count
    capacity = 2 * mean_load
    quarter = device_count // 4
    base = jax.random.fold_in(key, 7)
    key_map, key_rank, key_shift, key_order, key_rows, key_cols = jax.random.split(base, 6)
    slot_of = jax.random.permutation(key_map, NLIST).astype(jnp.int32)
    list_at = jnp.zeros((NLIST,), jnp.int32).at[slot_of].set(jnp.arange(NLIST, dtype=jnp.int32))
    ranked = jax.random.permutation(key_rank, device_count).astype(jnp.int32)
    shifts = jax.random.randint(key_shift, (device_count, quarter), 0, mean_load // 2 + 1).astype(jnp.int32)
    by_rank = jnp.concatenate([jnp.full((device_count, quarter), capacity, jnp.int32), 3 * mean_load // 2 - shifts, mean_load // 2 + shifts, jnp.zeros((device_count, device_count - 3 * quarter), jnp.int32)], axis=1)
    counts = jnp.zeros((device_count, device_count), jnp.int32).at[:, ranked].set(by_rank)
    orders = jax.vmap(lambda kk: jax.random.permutation(kk, device_count).astype(jnp.int32))(jax.random.split(key_order, device_count))
    row_keys = jax.random.split(key_rows, device_count)
    col_keys = jax.random.split(key_cols, device_count)

    def one_source(source, order_row, count_row, row_key, col_key):
        run_counts = count_row[order_row]
        target = jnp.repeat(order_row, run_counts, total_repeat_length=pair_count)
        starts = jnp.cumsum(run_counts) - run_counts
        run_index = jnp.repeat(jnp.arange(device_count, dtype=jnp.int32), run_counts, total_repeat_length=pair_count)
        within = jnp.arange(pair_count, dtype=jnp.int32) - starts[run_index]
        local = (source * capacity + within) % LISTS_DEV
        ids = list_at[target * LISTS_DEV + local]
        grid = ids.reshape(NPROBE, Q_DEV).T
        grid = grid[jax.random.permutation(row_key, Q_DEV)]
        grid = jax.vmap(lambda row, kk: row[jax.random.permutation(kk, NPROBE)])(grid, jax.random.split(col_key, Q_DEV))
        return grid
    grids = jax.vmap(one_source)(jnp.arange(device_count, dtype=jnp.int32), orders, counts, row_keys, col_keys)
    return (slot_of, grids.reshape(NQ, NPROBE).astype(jnp.int32))


def draw_probes(key, part):
    return probe_plan(key)[1]


def draw_owner_map(key, part):
    return probe_plan(key)[0]


def levels(stream_key, shape, shards, low, largest):
    gain = 1.0
    for dim, blocks in shards:
        heights = jax.random.uniform(jax.random.fold_in(jax.random.fold_in(stream_key, 6), dim), (blocks,), jnp.float32, low / len(shards), largest / len(shards))
        gain = gain * jnp.repeat(jnp.exp(heights), shape[dim] // blocks).reshape((-1,) + (1,) * (len(shape) - 1 - dim))
    return gain


def normal_values(rng, extent, width, reach, pieces=(), kind=jnp.bfloat16):
    values = width * jax.random.normal(rng, extent, jnp.float32)
    if pieces:
        values = values * levels(rng, extent, pieces, -0.22, 0.18)
    return jnp.clip(values, -reach, reach).astype(kind)


def setup_inputs(seed: int = 0) -> dict:
    splits = jax.random.split(jax.random.key(seed), 6)
    queries = normal_values(splits[0], (NQ, D), 1.0, 6.0, ((0, 32),))
    projection = normal_values(splits[1], (D, D), D ** -0.5, 0.21875)
    lists = normal_values(splits[2], (NLIST, LSIZE, D), 1.0, 6.0, ((0, 32),))
    probes = draw_probes(jax.random.fold_in(splits[5], 71), 0)
    owner_map = draw_owner_map(jax.random.fold_in(splits[5], 71), 0)
    return {"queries": queries, "projection": projection, "lists": lists, "probes": probes, "owner_map": owner_map}


def reference(queries, projection, lists, probes, owner_map):
    projected = jnp.dot(queries, projection, preferred_element_type=jnp.float32).astype(jnp.bfloat16)
    stored = jnp.take(owner_map, probes).astype(jnp.int32)
    block = 32
    query_blocks = projected.reshape(NQ // block, block, D)
    slot_blocks = stored.reshape(NQ // block, block, NPROBE)

    def one_block(args):
        rows, slots = args
        rows_f = rows.astype(jnp.float32)
        vectors = jnp.take(lists, slots.reshape(-1), axis=0).astype(jnp.float32)
        vectors = vectors.reshape(block, NPROBE, LSIZE, D)
        dots = jnp.einsum("qd,qjvd->qjv", rows_f, vectors)
        vec_norm = jnp.einsum("qjvd,qjvd->qjv", vectors, vectors)
        row_norm = jnp.sum(rows_f * rows_f, axis=1)
        return (row_norm[:, None, None] + vec_norm - 2.0 * dots) / D

    result = lax.map(one_block, (query_blocks, slot_blocks))
    return result.reshape(NQ, NPROBE, LSIZE)
```

```python
import jax
import jax.numpy as jnp
from jax import lax
from jax.sharding import PartitionSpec as P

AXES = ("grp", "own")


def body(queries, projection, lists, probes, owner_map):
    query_count, width = queries.shape
    probe_count = probes.shape[1]
    lists_here, list_size = lists.shape[0], lists.shape[1]
    device_count = lax.axis_size("grp") * lax.axis_size("own")
    pairs = query_count * probe_count
    capacity = 2 * pairs // device_count
    list_capacity = device_count * capacity // lists_here
    slots = device_count * capacity
    me = lax.axis_index(AXES)

    projected = jnp.dot(queries, projection, preferred_element_type=jnp.float32).astype(
        jnp.bfloat16
    )
    stored = jnp.take(owner_map, probes.reshape(-1))
    target = stored // lists_here
    local = stored % lists_here
    to_target = (target[:, None] == jnp.arange(device_count, dtype=jnp.int32)[None, :]).astype(
        jnp.bfloat16
    )
    step = jnp.arange(pairs, dtype=jnp.int32)
    earlier = (step[None, :] < step[:, None]).astype(jnp.bfloat16)
    before = jnp.dot(earlier, to_target, preferred_element_type=jnp.float32)
    rank = jnp.sum(before * to_target.astype(jnp.float32), axis=1).astype(jnp.int32)
    position = target * capacity + rank

    at_rank = (rank[:, None] == jnp.arange(capacity, dtype=jnp.int32)[None, :]).astype(jnp.bfloat16)
    query_of = step // probe_count
    what = jnp.stack([jnp.ones_like(step), query_of, local], axis=0).astype(jnp.bfloat16)
    weighted = to_target.T[None] * what[:, None, :]
    table = jnp.dot(
        weighted.reshape(3 * device_count, pairs), at_rank, preferred_element_type=jnp.float32
    ).reshape(3, device_count, capacity)
    table = jnp.where(table[:1] > 0.5, table[1:], -1.0).astype(jnp.bfloat16)
    extra = -(-(2 * slots) // width)
    extra = -(-extra // 16) * 16
    table = jnp.pad(table.reshape(-1), (0, extra * width - 2 * slots)).reshape(extra, width)

    everyone = lax.all_gather(jnp.concatenate([projected, table], axis=0), AXES, tiled=False)
    rows = everyone[:, :query_count].reshape(device_count * query_count, width)
    tables = everyone[:, query_count:].reshape(device_count, -1)[:, : 2 * slots]
    tables = tables.reshape(device_count, 2, device_count, capacity)
    mine = lax.dynamic_index_in_dim(tables, me, axis=2, keepdims=False).astype(jnp.int32)
    asked_query = mine[:, 0].reshape(-1)
    asked_list = mine[:, 1].reshape(-1)
    row_of = (
        asked_query + query_count * (jnp.arange(slots, dtype=jnp.int32) // capacity)
    )

    in_list = (asked_list[:, None] == jnp.arange(lists_here, dtype=jnp.int32)[None, :]).astype(
        jnp.bfloat16
    )
    place = jnp.arange(slots, dtype=jnp.int32)
    earlier = (place[None, :] < place[:, None]).astype(jnp.bfloat16)
    before = jnp.dot(earlier, in_list, preferred_element_type=jnp.float32)
    order = jnp.sum(before * in_list.astype(jnp.float32), axis=1).astype(jnp.int32)
    valid = asked_list >= 0
    spot = jnp.where(valid, asked_list * list_capacity + order, -1)
    hit = spot[:, None] == jnp.arange(lists_here * list_capacity, dtype=jnp.int32)[None, :]
    grouped_row = jnp.sum(jnp.where(hit, row_of[:, None], 0), axis=0)
    grouped = rows[grouped_row].reshape(lists_here, list_capacity, width)

    dots = jnp.einsum("lcd,lvd->lcv", grouped, lists, preferred_element_type=jnp.float32)
    vec_norm = jnp.einsum("lvd,lvd->lv", lists, lists, preferred_element_type=jnp.float32)
    row_norm = jnp.einsum("lcd,lcd->lc", grouped, grouped, preferred_element_type=jnp.float32)
    distance = (row_norm[:, :, None] + vec_norm[:, None, :] - 2.0 * dots) / width
    flat_dist = distance.reshape(lists_here * list_capacity, list_size)
    answers = flat_dist[jnp.maximum(spot, 0)]
    returned = lax.all_to_all(
        answers.reshape(device_count, capacity, list_size),
        AXES,
        split_axis=0,
        concat_axis=0,
        tiled=True,
    )
    returned = returned.reshape(slots, list_size)
    return returned[position].reshape(query_count, probe_count, list_size)


def solution(mesh):
    placed = (
        P(AXES, None),
        P(),
        P(AXES, None, None),
        P(AXES, None),
        P(),
    )
    return jax.shard_map(
        body, mesh=mesh, in_specs=placed, out_specs=P(AXES, None, None), check_vma=False
    )
```

```python
import jax
import jax.numpy as jnp
from jax import lax
from jax.experimental import pallas as pl
from jax.experimental.pallas import tpu as pltpu
from jax.sharding import PartitionSpec as P

AXES = ("grp", "own")
LANES = 128


def gather_kernel(mine_ref, all_ref, send_sem, recv_sem):
    grp, own = lax.axis_index("grp"), lax.axis_index("own")
    z, x, y, c = grp // 2, grp % 2, own // 2, own % 2

    def device(zz, xx, yy, cc):
        return (zz * 2 + xx, yy * 2 + cc)

    def number(zz, xx, yy, cc):
        return (zz * 2 + xx) * 4 + yy * 2 + cc

    zs = [z] + [lax.rem(z + k, 4) for k in (1, 2, 3)]
    over_z = [device(zz, x, y, c) for zz in zs[1:]]
    over_x, over_y = device(z, 1 - x, y, c), device(z, x, 1 - y, c)
    sibling = device(z, x, y, 1 - c)
    barrier = pltpu.get_barrier_semaphore()
    for peer in over_z + [over_x, over_y, sibling]:
        pl.semaphore_signal(barrier, inc=1, device_id=peer, device_id_type=pl.DeviceIdType.MESH)
    pl.semaphore_wait(barrier, 6)

    sent = []

    def describe(src, block, peer, slot):
        return pltpu.make_async_remote_copy(
            src_ref=src,
            dst_ref=all_ref.at[block],
            send_sem=send_sem.at[slot],
            recv_sem=recv_sem.at[block],
            device_id=peer,
            device_id_type=pl.DeviceIdType.MESH,
        )

    def send(src, block, peer):
        copy = describe(src, block, peer, len(sent))
        copy.start()
        sent.append(copy)

    def arrived(block):
        describe(all_ref.at[block], block, sibling, 0).wait_recv()
        return all_ref.at[block]

    me = number(z, x, y, c)
    for peer in over_z + [over_x, over_y, sibling]:
        send(mine_ref, me, peer)
    all_ref[me] = mine_ref[...]
    for k in (0, 1, 3, 2):
        if k:
            block = number(zs[k], x, y, c)
            ref = arrived(block)
            for peer in (over_x, over_y, sibling):
                send(ref, block, peer)
        block = number(zs[k], 1 - x, y, c)
        ref = arrived(block)
        if k % 2 == 1:
            send(ref, block, over_y)
        send(ref, block, sibling)
        block = number(zs[k], x, 1 - y, c)
        ref = arrived(block)
        if k % 2 == 0:
            send(ref, block, over_x)
        send(ref, block, sibling)
    for k in (0, 1, 3, 2):
        block = number(zs[k], 1 - x, 1 - y, c)
        send(arrived(block), block, sibling)
    for k in (0, 1, 3, 2):
        for xx in (x, 1 - x):
            for yy in (y, 1 - y):
                arrived(number(zs[k], xx, yy, 1 - c))
    for copy in sent:
        copy.wait_send()


def gather_all(block):
    group_count, owner_count = lax.axis_size("grp"), lax.axis_size("own")
    if (group_count, owner_count) != (8, 4):
        return lax.all_gather(block, AXES, tiled=False)
    device_count = group_count * owner_count
    return pl.pallas_call(
        gather_kernel,
        out_shape=jax.ShapeDtypeStruct((device_count,) + block.shape, block.dtype),
        in_specs=[pl.BlockSpec(memory_space=pltpu.VMEM)],
        out_specs=pl.BlockSpec(memory_space=pltpu.VMEM),
        scratch_shapes=[
            pltpu.SemaphoreType.DMA((device_count,)),
            pltpu.SemaphoreType.DMA((device_count,)),
        ],
        compiler_params=pltpu.CompilerParams(
            collective_id=0, has_side_effects=True, vmem_limit_bytes=16 * 2**20
        ),
    )(block)


def body(queries, projection, lists, probes, owner_map):
    query_count, width = queries.shape
    probe_count = probes.shape[1]
    lists_here, list_size = lists.shape[0], lists.shape[1]
    device_count = lax.axis_size("grp") * lax.axis_size("own")
    pairs = query_count * probe_count
    capacity = 2 * pairs // device_count
    list_capacity = device_count * capacity // lists_here
    slots = device_count * capacity
    me = lax.axis_index(AXES)

    projected = jnp.dot(queries, projection, preferred_element_type=jnp.float32).astype(
        jnp.bfloat16
    )
    stored = jnp.take(owner_map, probes.reshape(-1))
    target = stored // lists_here
    local = stored % lists_here
    to_target = (target[:, None] == jnp.arange(device_count, dtype=jnp.int32)[None, :]).astype(
        jnp.bfloat16
    )
    step = jnp.arange(pairs, dtype=jnp.int32)
    earlier = (step[None, :] < step[:, None]).astype(jnp.bfloat16)
    before = jnp.dot(earlier, to_target, preferred_element_type=jnp.float32)
    rank = jnp.sum(before * to_target.astype(jnp.float32), axis=1).astype(jnp.int32)
    position = target * capacity + rank

    at_rank = (rank[:, None] == jnp.arange(capacity, dtype=jnp.int32)[None, :]).astype(jnp.bfloat16)
    query_of = step // probe_count
    what = jnp.stack([jnp.ones_like(step), query_of, local], axis=0).astype(jnp.bfloat16)
    weighted = to_target.T[None] * what[:, None, :]
    table = jnp.dot(
        weighted.reshape(3 * device_count, pairs), at_rank, preferred_element_type=jnp.float32
    ).reshape(3, device_count, capacity)
    table = jnp.where(table[:1] > 0.5, table[1:], -1.0).astype(jnp.bfloat16)
    columns = width // LANES
    extra = -(-(2 * slots) // (16 * LANES)) * 16
    table = jnp.pad(table.reshape(-1), (0, extra * LANES - 2 * slots)).reshape(extra, LANES)
    stacked = projected.reshape(query_count, columns, LANES).transpose(1, 0, 2)
    stacked = stacked.reshape(columns * query_count, LANES)

    everyone = gather_all(jnp.concatenate([stacked, table], axis=0))
    rows = everyone[:, : columns * query_count].reshape(
        device_count, columns, query_count, LANES
    )
    rows = rows.transpose(0, 2, 1, 3).reshape(device_count * query_count, width)
    tables = everyone[:, columns * query_count :].reshape(device_count, -1)[:, : 2 * slots]
    tables = tables.reshape(device_count, 2, device_count, capacity)
    mine = lax.dynamic_index_in_dim(tables, me, axis=2, keepdims=False).astype(jnp.int32)
    asked_query = mine[:, 0].reshape(-1)
    asked_list = mine[:, 1].reshape(-1)
    row_of = (
        asked_query + query_count * (jnp.arange(slots, dtype=jnp.int32) // capacity)
    )

    in_list = (asked_list[:, None] == jnp.arange(lists_here, dtype=jnp.int32)[None, :]).astype(
        jnp.bfloat16
    )
    place = jnp.arange(slots, dtype=jnp.int32)
    earlier = (place[None, :] < place[:, None]).astype(jnp.bfloat16)
    before = jnp.dot(earlier, in_list, preferred_element_type=jnp.float32)
    order = jnp.sum(before * in_list.astype(jnp.float32), axis=1).astype(jnp.int32)
    valid = asked_list >= 0
    spot = jnp.where(valid, asked_list * list_capacity + order, -1)
    hit = spot[:, None] == jnp.arange(lists_here * list_capacity, dtype=jnp.int32)[None, :]
    grouped_row = jnp.sum(jnp.where(hit, row_of[:, None], 0), axis=0)
    grouped = rows[grouped_row].reshape(lists_here, list_capacity, width)

    dots = jnp.einsum("lcd,lvd->lcv", grouped, lists, preferred_element_type=jnp.float32)
    vec_norm = jnp.einsum("lvd,lvd->lv", lists, lists, preferred_element_type=jnp.float32)
    row_norm = jnp.einsum("lcd,lcd->lc", grouped, grouped, preferred_element_type=jnp.float32)
    distance = (row_norm[:, :, None] + vec_norm[:, None, :] - 2.0 * dots) / width
    flat_dist = distance.reshape(lists_here * list_capacity, list_size)
    answers = flat_dist[jnp.maximum(spot, 0)]
    returned = lax.all_to_all(
        answers.reshape(device_count, capacity, list_size),
        AXES,
        split_axis=0,
        concat_axis=0,
        tiled=True,
    )
    returned = returned.reshape(slots, list_size)
    return returned[position].reshape(query_count, probe_count, list_size)


def solution(mesh):
    placed = (
        P(AXES, None),
        P(),
        P(AXES, None, None),
        P(AXES, None),
        P(),
    )
    return jax.shard_map(
        body, mesh=mesh, in_specs=placed, out_specs=P(AXES, None, None), check_vma=False
    )
```

```python
import jax
import jax.numpy as jnp
from jax import lax
from jax.experimental import pallas as pl
from jax.experimental.pallas import tpu as pltpu
from jax.sharding import PartitionSpec as P

AXES = ("grp", "own")
LANES = 128


def gather_kernel(mine_ref, all_ref, send_sem, recv_sem):
    grp, own = lax.axis_index("grp"), lax.axis_index("own")
    z, x, y, c = grp // 2, grp % 2, own // 2, own % 2

    def device(zz, xx, yy, cc):
        return (zz * 2 + xx, yy * 2 + cc)

    def number(zz, xx, yy, cc):
        return (zz * 2 + xx) * 4 + yy * 2 + cc

    zs = [z] + [lax.rem(z + k, 4) for k in (1, 2, 3)]
    over_z = [device(zz, x, y, c) for zz in zs[1:]]
    over_x, over_y = device(z, 1 - x, y, c), device(z, x, 1 - y, c)
    sibling = device(z, x, y, 1 - c)
    barrier = pltpu.get_barrier_semaphore()
    for peer in over_z + [over_x, over_y, sibling]:
        pl.semaphore_signal(barrier, inc=1, device_id=peer, device_id_type=pl.DeviceIdType.MESH)
    pl.semaphore_wait(barrier, 6)

    sent = []

    def describe(src, block, peer, slot):
        return pltpu.make_async_remote_copy(
            src_ref=src,
            dst_ref=all_ref.at[block],
            send_sem=send_sem.at[slot],
            recv_sem=recv_sem.at[block],
            device_id=peer,
            device_id_type=pl.DeviceIdType.MESH,
        )

    def send(src, block, peer):
        copy = describe(src, block, peer, len(sent))
        copy.start()
        sent.append(copy)

    def arrived(block):
        describe(all_ref.at[block], block, sibling, 0).wait_recv()
        return all_ref.at[block]

    me = number(z, x, y, c)
    for peer in over_z + [over_x, over_y, sibling]:
        send(mine_ref, me, peer)
    all_ref[me] = mine_ref[...]
    for k in (0, 1, 3, 2):
        if k:
            block = number(zs[k], x, y, c)
            ref = arrived(block)
            for peer in (over_x, over_y, sibling):
                send(ref, block, peer)
        block = number(zs[k], 1 - x, y, c)
        ref = arrived(block)
        if k % 2 == 1:
            send(ref, block, over_y)
        send(ref, block, sibling)
        block = number(zs[k], x, 1 - y, c)
        ref = arrived(block)
        if k % 2 == 0:
            send(ref, block, over_x)
        send(ref, block, sibling)
    for k in (0, 1, 3, 2):
        block = number(zs[k], 1 - x, 1 - y, c)
        send(arrived(block), block, sibling)
    for k in (0, 1, 3, 2):
        for xx in (x, 1 - x):
            for yy in (y, 1 - y):
                arrived(number(zs[k], xx, yy, 1 - c))
    for copy in sent:
        copy.wait_send()


def gather_all(block):
    group_count, owner_count = lax.axis_size("grp"), lax.axis_size("own")
    if (group_count, owner_count) != (8, 4):
        return lax.all_gather(block, AXES, tiled=False)
    device_count = group_count * owner_count
    return pl.pallas_call(
        gather_kernel,
        out_shape=jax.ShapeDtypeStruct((device_count,) + block.shape, block.dtype),
        in_specs=[pl.BlockSpec(memory_space=pltpu.VMEM)],
        out_specs=pl.BlockSpec(memory_space=pltpu.VMEM),
        scratch_shapes=[
            pltpu.SemaphoreType.DMA((device_count,)),
            pltpu.SemaphoreType.DMA((device_count,)),
        ],
        compiler_params=pltpu.CompilerParams(
            collective_id=0, has_side_effects=True, vmem_limit_bytes=16 * 2**20
        ),
    )(block)


def select_kernel(queries, width, row_ref, all_ref, out_ref):
    devices = all_ref.shape[0]
    count = out_ref.shape[0]
    numbers = lax.broadcasted_iota(jnp.int32, (count, devices * queries), 1)
    pick = (numbers == row_ref[...]).astype(jnp.float32).astype(jnp.bfloat16)
    for j in range(width // LANES):
        part = all_ref[:, j * queries : (j + 1) * queries, :].reshape(devices * queries, LANES)
        out_ref[:, j * LANES : (j + 1) * LANES] = jnp.dot(
            pick, part, preferred_element_type=jnp.float32
        ).astype(jnp.bfloat16)


def select_rows(everyone, row_of, queries, width):
    slots = row_of.shape[0]
    block = min(256, slots)
    return pl.pallas_call(
        lambda *refs: select_kernel(queries, width, *refs),
        grid=(slots // block,),
        out_shape=jax.ShapeDtypeStruct((slots, width), jnp.bfloat16),
        in_specs=[
            pl.BlockSpec((block, 1), lambda i: (i, 0)),
            pl.BlockSpec(memory_space=pltpu.VMEM),
        ],
        out_specs=pl.BlockSpec((block, width), lambda i: (i, 0)),
        compiler_params=pltpu.CompilerParams(vmem_limit_bytes=48 * 2**20),
    )(row_of[:, None], everyone)


def exchange_kernel(device_count, owner_count, out_ref, in_ref, send_sem, recv_sem):
    me = lax.axis_index("grp") * owner_count + lax.axis_index("own")

    def at(k):
        other = lax.rem(me + k, device_count)
        return other, (other // owner_count, lax.rem(other, owner_count))

    barrier = pltpu.get_barrier_semaphore()

    @pl.loop(1, device_count)
    def _(k):
        pl.semaphore_signal(
            barrier, inc=1, device_id=at(k)[1], device_id_type=pl.DeviceIdType.MESH
        )

    pl.semaphore_wait(barrier, device_count - 1)

    def describe(k, block):
        other, where = at(k)
        return pltpu.make_async_remote_copy(
            src_ref=out_ref.at[other],
            dst_ref=in_ref.at[block],
            send_sem=send_sem.at[k],
            recv_sem=recv_sem.at[block],
            device_id=where,
            device_id_type=pl.DeviceIdType.MESH,
        )

    @pl.loop(1, device_count)
    def _(k):
        describe(k, me).start()

    in_ref[me] = out_ref[me]

    @pl.loop(1, device_count)
    def _(k):
        describe(k, at(k)[0]).wait_recv()

    @pl.loop(1, device_count)
    def _(k):
        describe(k, me).wait_send()


def exchange(blocks):
    owner_count = lax.axis_size("own")
    device_count = blocks.shape[0]
    return pl.pallas_call(
        lambda *refs: exchange_kernel(device_count, owner_count, *refs),
        out_shape=jax.ShapeDtypeStruct(blocks.shape, blocks.dtype),
        in_specs=[pl.BlockSpec(memory_space=pltpu.VMEM)],
        out_specs=pl.BlockSpec(memory_space=pltpu.VMEM),
        scratch_shapes=[
            pltpu.SemaphoreType.DMA((device_count,)),
            pltpu.SemaphoreType.DMA((device_count,)),
        ],
        compiler_params=pltpu.CompilerParams(
            collective_id=1, has_side_effects=True, vmem_limit_bytes=16 * 2**20
        ),
    )(blocks)


def body(queries, projection, lists, probes, owner_map):
    query_count, width = queries.shape
    probe_count = probes.shape[1]
    lists_here, list_size = lists.shape[0], lists.shape[1]
    device_count = lax.axis_size("grp") * lax.axis_size("own")
    pairs = query_count * probe_count
    capacity = 2 * pairs // device_count
    list_capacity = device_count * capacity // lists_here
    slots = device_count * capacity
    me = lax.axis_index(AXES)

    projected = jnp.dot(queries, projection, preferred_element_type=jnp.float32).astype(
        jnp.bfloat16
    )
    stored = jnp.take(owner_map, probes.reshape(-1))
    target = stored // lists_here
    local = stored % lists_here
    to_target = (target[:, None] == jnp.arange(device_count, dtype=jnp.int32)[None, :]).astype(
        jnp.bfloat16
    )
    step = jnp.arange(pairs, dtype=jnp.int32)
    earlier = (step[None, :] < step[:, None]).astype(jnp.bfloat16)
    before = jnp.dot(earlier, to_target, preferred_element_type=jnp.float32)
    rank = jnp.sum(before * to_target.astype(jnp.float32), axis=1).astype(jnp.int32)
    position = target * capacity + rank

    at_rank = (rank[:, None] == jnp.arange(capacity, dtype=jnp.int32)[None, :]).astype(jnp.bfloat16)
    query_of = step // probe_count
    what = jnp.stack([jnp.ones_like(step), query_of, local], axis=0).astype(jnp.bfloat16)
    weighted = to_target.T[None] * what[:, None, :]
    table = jnp.dot(
        weighted.reshape(3 * device_count, pairs), at_rank, preferred_element_type=jnp.float32
    ).reshape(3, device_count, capacity)
    table = jnp.where(table[:1] > 0.5, table[1:], -1.0).astype(jnp.bfloat16)
    columns = width // LANES
    extra = -(-(2 * slots) // (16 * LANES)) * 16
    table = jnp.pad(table.reshape(-1), (0, extra * LANES - 2 * slots)).reshape(extra, LANES)
    stacked = projected.reshape(query_count, columns, LANES).transpose(1, 0, 2)
    stacked = stacked.reshape(columns * query_count, LANES)

    everyone = gather_all(jnp.concatenate([stacked, table], axis=0))
    tables = everyone[:, columns * query_count :].reshape(device_count, -1)[:, : 2 * slots]
    tables = tables.reshape(device_count, 2, device_count, capacity)
    mine = lax.dynamic_index_in_dim(tables, me, axis=2, keepdims=False).astype(jnp.int32)
    asked_query = mine[:, 0].reshape(-1)
    asked_list = mine[:, 1].reshape(-1)
    row_of = (
        asked_query + query_count * (jnp.arange(slots, dtype=jnp.int32) // capacity)
    )

    in_list = (asked_list[:, None] == jnp.arange(lists_here, dtype=jnp.int32)[None, :]).astype(
        jnp.bfloat16
    )
    place = jnp.arange(slots, dtype=jnp.int32)
    earlier = (place[None, :] < place[:, None]).astype(jnp.bfloat16)
    before = jnp.dot(earlier, in_list, preferred_element_type=jnp.float32)
    order = jnp.sum(before * in_list.astype(jnp.float32), axis=1).astype(jnp.int32)
    valid = asked_list >= 0
    spot = jnp.where(valid, asked_list * list_capacity + order, -1)
    hit = spot[:, None] == jnp.arange(lists_here * list_capacity, dtype=jnp.int32)[None, :]
    grouped_row = jnp.sum(jnp.where(hit, row_of[:, None], 0), axis=0)
    grouped = select_rows(everyone, grouped_row, query_count, width)
    grouped = grouped.reshape(lists_here, list_capacity, width)

    dots = jnp.einsum("lcd,lvd->lcv", grouped, lists, preferred_element_type=jnp.float32)
    vec_norm = jnp.einsum("lvd,lvd->lv", lists, lists, preferred_element_type=jnp.float32)
    row_norm = jnp.einsum("lcd,lcd->lc", grouped, grouped, preferred_element_type=jnp.float32)
    distance = (row_norm[:, :, None] + vec_norm[:, None, :] - 2.0 * dots) / width
    flat_dist = distance.reshape(lists_here * list_capacity, list_size)
    largest = jnp.max(jnp.abs(flat_dist), axis=1, keepdims=True)
    power = jnp.clip(jnp.ceil(jnp.log2(largest) + 1e-3), -120.0, 120.0)
    codes = jnp.round(jnp.maximum(flat_dist, 0.0) * (65535.0 * jnp.exp2(-power))) - 32768.0
    codes = jnp.clip(codes, -32768.0, 32767.0)
    coded = jnp.concatenate(
        [codes, jnp.broadcast_to(power, (power.shape[0], LANES))], axis=1
    )[jnp.maximum(spot, 0)]
    answer_rows = capacity * list_size // LANES
    power_rows = -(-capacity // (16 * LANES)) * 16
    powers = jnp.pad(
        coded[:, list_size].reshape(device_count, capacity),
        ((0, 0), (0, power_rows * LANES - capacity)),
    )
    blocks = jnp.concatenate(
        [
            coded[:, :list_size]
            .reshape(device_count, capacity, list_size // LANES, LANES)
            .transpose(0, 2, 1, 3)
            .reshape(device_count, answer_rows, LANES),
            powers.reshape(device_count, power_rows, LANES),
        ],
        axis=1,
    ).astype(jnp.int16)
    got = exchange(blocks).astype(jnp.float32)
    powers = got[:, answer_rows:].reshape(device_count, -1)[:, :capacity].reshape(slots, 1)
    returned = (
        got[:, :answer_rows]
        .reshape(device_count, list_size // LANES, capacity, LANES)
        .transpose(0, 2, 1, 3)
        .reshape(slots, list_size)
    )
    returned = (returned + 32768.0) * (jnp.exp2(powers) / 65535.0)
    return returned[position].reshape(query_count, probe_count, list_size)


def solution(mesh):
    placed = (
        P(AXES, None),
        P(),
        P(AXES, None, None),
        P(AXES, None),
        P(),
    )
    return jax.shard_map(
        body, mesh=mesh, in_specs=placed, out_specs=P(AXES, None, None), check_vma=False
    )
```

```python
import jax
import jax.numpy as jnp
from jax import lax
from jax.experimental import pallas as pl
from jax.experimental.pallas import tpu as pltpu
from jax.sharding import PartitionSpec as P

AXES = ("grp", "own")
LANES = 128
LOG2E = 1.4426950408889634
LN2 = 0.6931471805599453


def gather_kernel(mine_ref, all_ref, send_sem, recv_sem):
    grp, own = lax.axis_index("grp"), lax.axis_index("own")
    z, x, y, c = grp // 2, grp % 2, own // 2, own % 2

    def device(zz, xx, yy, cc):
        return (zz * 2 + xx, yy * 2 + cc)

    def number(zz, xx, yy, cc):
        return (zz * 2 + xx) * 4 + yy * 2 + cc

    zs = [z] + [lax.rem(z + k, 4) for k in (1, 2, 3)]
    over_z = [device(zz, x, y, c) for zz in zs[1:]]
    over_x, over_y = device(z, 1 - x, y, c), device(z, x, 1 - y, c)
    sibling = device(z, x, y, 1 - c)
    barrier = pltpu.get_barrier_semaphore()
    for peer in over_z + [over_x, over_y, sibling]:
        pl.semaphore_signal(barrier, inc=1, device_id=peer, device_id_type=pl.DeviceIdType.MESH)
    pl.semaphore_wait(barrier, 6)

    sent = []

    def describe(src, block, peer, slot):
        return pltpu.make_async_remote_copy(
            src_ref=src,
            dst_ref=all_ref.at[block],
            send_sem=send_sem.at[slot],
            recv_sem=recv_sem.at[block],
            device_id=peer,
            device_id_type=pl.DeviceIdType.MESH,
        )

    def send(src, block, peer):
        copy = describe(src, block, peer, len(sent))
        copy.start()
        sent.append(copy)

    def arrived(block):
        describe(all_ref.at[block], block, sibling, 0).wait_recv()
        return all_ref.at[block]

    me = number(z, x, y, c)
    for peer in over_z + [over_x, over_y, sibling]:
        send(mine_ref, me, peer)
    all_ref[me] = mine_ref[...]
    for k in (0, 1, 3, 2):
        if k:
            block = number(zs[k], x, y, c)
            ref = arrived(block)
            for peer in (over_x, over_y, sibling):
                send(ref, block, peer)
        block = number(zs[k], 1 - x, y, c)
        ref = arrived(block)
        if k % 2 == 1:
            send(ref, block, over_y)
        send(ref, block, sibling)
        block = number(zs[k], x, 1 - y, c)
        ref = arrived(block)
        if k % 2 == 0:
            send(ref, block, over_x)
        send(ref, block, sibling)
    for k in (0, 1, 3, 2):
        block = number(zs[k], 1 - x, 1 - y, c)
        send(arrived(block), block, sibling)
    for k in (0, 1, 3, 2):
        for xx in (x, 1 - x):
            for yy in (y, 1 - y):
                arrived(number(zs[k], xx, yy, 1 - c))
    for copy in sent:
        copy.wait_send()


def gather_all(block):
    group_count, owner_count = lax.axis_size("grp"), lax.axis_size("own")
    if (group_count, owner_count) != (8, 4):
        return lax.all_gather(block, AXES, tiled=False)
    device_count = group_count * owner_count
    return pl.pallas_call(
        gather_kernel,
        out_shape=jax.ShapeDtypeStruct((device_count,) + block.shape, block.dtype),
        in_specs=[pl.BlockSpec(memory_space=pltpu.VMEM)],
        out_specs=pl.BlockSpec(memory_space=pltpu.VMEM),
        scratch_shapes=[
            pltpu.SemaphoreType.DMA((device_count,)),
            pltpu.SemaphoreType.DMA((device_count,)),
        ],
        compiler_params=pltpu.CompilerParams(
            collective_id=0, has_side_effects=True, vmem_limit_bytes=16 * 2**20
        ),
    )(block)


def select_kernel(queries, width, row_ref, all_ref, out_ref):
    devices = all_ref.shape[0]
    count = out_ref.shape[0]
    numbers = lax.broadcasted_iota(jnp.int32, (count, devices * queries), 1)
    pick = (numbers == row_ref[...]).astype(jnp.float32).astype(jnp.bfloat16)
    for j in range(width // LANES):
        part = all_ref[:, j * queries : (j + 1) * queries, :].reshape(devices * queries, LANES)
        out_ref[:, j * LANES : (j + 1) * LANES] = jnp.dot(
            pick, part, preferred_element_type=jnp.float32
        ).astype(jnp.bfloat16)


def select_rows(everyone, row_of, queries, width):
    slots = row_of.shape[0]
    block = min(256, slots)
    return pl.pallas_call(
        lambda *refs: select_kernel(queries, width, *refs),
        grid=(slots // block,),
        out_shape=jax.ShapeDtypeStruct((slots, width), jnp.bfloat16),
        in_specs=[
            pl.BlockSpec((block, 1), lambda i: (i, 0)),
            pl.BlockSpec(memory_space=pltpu.VMEM),
        ],
        out_specs=pl.BlockSpec((block, width), lambda i: (i, 0)),
        compiler_params=pltpu.CompilerParams(vmem_limit_bytes=48 * 2**20),
    )(row_of[:, None], everyone)


def score_kernel(blocks, rows_ref, lists_ref, spot_ref, out_ref, held):
    step = pl.program_id(0)
    count, list_size, width = lists_ref.shape
    capacity = rows_ref.shape[0] // count
    for n in range(count):
        rows = rows_ref[n * capacity : (n + 1) * capacity, :]
        dots = lax.dot_general(
            rows, lists_ref[n], (((1,), (1,)), ((), ())), preferred_element_type=jnp.float32
        )
        rows_f = rows.astype(jnp.float32)
        row_norm = jnp.sum(rows_f * rows_f, axis=1, keepdims=True)
        partial = None
        for j in range(width // LANES):
            part = lists_ref[n, :, j * LANES : (j + 1) * LANES].astype(jnp.float32)
            partial = part * part if partial is None else partial + part * part
        vec_norm = jnp.sum(partial.T, axis=0, keepdims=True)
        distance = jnp.maximum((row_norm + vec_norm - 2.0 * dots) / width, 0.0)
        largest = jnp.maximum(jnp.max(distance, axis=1, keepdims=True), 1e-30)
        power = jnp.clip(jnp.ceil(jnp.log(largest) * LOG2E + 1e-3), -100.0, 120.0)
        code = jnp.clip(jnp.round(distance * (65535.0 * jnp.exp(power * -LN2))), 0.0, 65535.0)
        high = jnp.floor(code * (1.0 / 256.0))
        low = code - high * 256.0
        place = pl.ds(pl.multiple_of((step * count + n) * capacity, 16), capacity)
        held[place, :list_size] = high.astype(jnp.bfloat16)
        held[place, list_size : 2 * list_size] = low.astype(jnp.bfloat16)
        held[place, 2 * list_size :] = jnp.broadcast_to(power, (capacity, LANES)).astype(
            jnp.bfloat16
        )

    @pl.when(step == pl.num_programs(0) - 1)
    def _():
        slots = held.shape[0]
        each = slots // blocks
        numbers = lax.broadcasted_iota(jnp.int32, (slots, slots), 1)
        pick = (numbers == spot_ref[...]).astype(jnp.float32).astype(jnp.bfloat16)
        got = jnp.dot(pick, held[...], preferred_element_type=jnp.float32)
        code = got[:, :list_size] * 256.0 + got[:, list_size : 2 * list_size] - 32768.0
        parts = [
            code[:, h * LANES : (h + 1) * LANES].reshape(blocks, each, LANES)
            for h in range(list_size // LANES)
        ]
        powers = got[:, 2 * list_size :].reshape(blocks, each, LANES)
        slot = lax.broadcasted_iota(jnp.int32, powers.shape, 1)
        lane = lax.broadcasted_iota(jnp.int32, powers.shape, 2)
        powers = jnp.sum(jnp.where(slot == lane, powers, 0.0), axis=1, keepdims=True)
        parts.append(jnp.broadcast_to(powers, (blocks, 16, LANES)))
        whole = jnp.concatenate(parts, axis=1)
        out_ref[...] = whole.astype(jnp.int32).astype(jnp.int16)


def score(grouped, lists, spot, blocks):
    list_count, list_size, width = lists.shape
    slots = grouped.shape[0]
    count = 4
    out_rows = (slots // blocks) * list_size // LANES + 16
    return pl.pallas_call(
        lambda *refs: score_kernel(blocks, *refs),
        grid=(list_count // count,),
        out_shape=jax.ShapeDtypeStruct((blocks, out_rows, LANES), jnp.int16),
        in_specs=[
            pl.BlockSpec((slots // list_count * count, width), lambda i: (i, 0)),
            pl.BlockSpec((count, list_size, width), lambda i: (i, 0, 0)),
            pl.BlockSpec((slots, 1), lambda i: (0, 0)),
        ],
        out_specs=pl.BlockSpec((blocks, out_rows, LANES), lambda i: (0, 0, 0)),
        scratch_shapes=[pltpu.VMEM((slots, 2 * list_size + LANES), jnp.bfloat16)],
        compiler_params=pltpu.CompilerParams(vmem_limit_bytes=40 * 2**20),
    )(grouped, lists, spot[:, None])


def exchange_kernel(device_count, owner_count, out_ref, in_ref, send_sem, recv_sem):
    me = lax.axis_index("grp") * owner_count + lax.axis_index("own")

    def at(k):
        other = lax.rem(me + k, device_count)
        return other, (other // owner_count, lax.rem(other, owner_count))

    barrier = pltpu.get_barrier_semaphore()

    @pl.loop(1, device_count)
    def _(k):
        pl.semaphore_signal(
            barrier, inc=1, device_id=at(k)[1], device_id_type=pl.DeviceIdType.MESH
        )

    pl.semaphore_wait(barrier, device_count - 1)

    def describe(k, block):
        other, where = at(k)
        return pltpu.make_async_remote_copy(
            src_ref=out_ref.at[other],
            dst_ref=in_ref.at[block],
            send_sem=send_sem.at[k],
            recv_sem=recv_sem.at[block],
            device_id=where,
            device_id_type=pl.DeviceIdType.MESH,
        )

    @pl.loop(1, device_count)
    def _(k):
        describe(k, me).start()

    in_ref[me] = out_ref[me]

    @pl.loop(1, device_count)
    def _(k):
        describe(k, at(k)[0]).wait_recv()

    @pl.loop(1, device_count)
    def _(k):
        describe(k, me).wait_send()


def exchange(blocks):
    owner_count = lax.axis_size("own")
    device_count = blocks.shape[0]
    return pl.pallas_call(
        lambda *refs: exchange_kernel(device_count, owner_count, *refs),
        out_shape=jax.ShapeDtypeStruct(blocks.shape, blocks.dtype),
        in_specs=[pl.BlockSpec(memory_space=pltpu.VMEM)],
        out_specs=pl.BlockSpec(memory_space=pltpu.VMEM),
        scratch_shapes=[
            pltpu.SemaphoreType.DMA((device_count,)),
            pltpu.SemaphoreType.DMA((device_count,)),
        ],
        compiler_params=pltpu.CompilerParams(
            collective_id=1, has_side_effects=True, vmem_limit_bytes=16 * 2**20
        ),
    )(blocks)


def body(queries, projection, lists, probes, owner_map):
    query_count, width = queries.shape
    probe_count = probes.shape[1]
    lists_here, list_size = lists.shape[0], lists.shape[1]
    device_count = lax.axis_size("grp") * lax.axis_size("own")
    pairs = query_count * probe_count
    capacity = 2 * pairs // device_count
    list_capacity = device_count * capacity // lists_here
    slots = device_count * capacity
    me = lax.axis_index(AXES)

    projected = jnp.dot(queries, projection, preferred_element_type=jnp.float32).astype(
        jnp.bfloat16
    )
    stored = jnp.take(owner_map, probes.reshape(-1))
    target = stored // lists_here
    local = stored % lists_here
    to_target = (target[:, None] == jnp.arange(device_count, dtype=jnp.int32)[None, :]).astype(
        jnp.bfloat16
    )
    step = jnp.arange(pairs, dtype=jnp.int32)
    earlier = (step[None, :] < step[:, None]).astype(jnp.bfloat16)
    before = jnp.dot(earlier, to_target, preferred_element_type=jnp.float32)
    rank = jnp.sum(before * to_target.astype(jnp.float32), axis=1).astype(jnp.int32)
    position = target * capacity + rank

    at_rank = (rank[:, None] == jnp.arange(capacity, dtype=jnp.int32)[None, :]).astype(jnp.bfloat16)
    query_of = step // probe_count
    what = jnp.stack([jnp.ones_like(step), query_of, local], axis=0).astype(jnp.bfloat16)
    weighted = to_target.T[None] * what[:, None, :]
    table = jnp.dot(
        weighted.reshape(3 * device_count, pairs), at_rank, preferred_element_type=jnp.float32
    ).reshape(3, device_count, capacity)
    table = jnp.where(table[:1] > 0.5, table[1:], -1.0).astype(jnp.bfloat16)
    columns = width // LANES
    extra = -(-(2 * slots) // (16 * LANES)) * 16
    table = jnp.pad(table.reshape(-1), (0, extra * LANES - 2 * slots)).reshape(extra, LANES)
    stacked = projected.reshape(query_count, columns, LANES).transpose(1, 0, 2)
    stacked = stacked.reshape(columns * query_count, LANES)

    everyone = gather_all(jnp.concatenate([stacked, table], axis=0))
    tables = everyone[:, columns * query_count :].reshape(device_count, -1)[:, : 2 * slots]
    tables = tables.reshape(device_count, 2, device_count, capacity)
    mine = lax.dynamic_index_in_dim(tables, me, axis=2, keepdims=False).astype(jnp.int32)
    asked_query = mine[:, 0].reshape(-1)
    asked_list = mine[:, 1].reshape(-1)
    row_of = (
        asked_query + query_count * (jnp.arange(slots, dtype=jnp.int32) // capacity)
    )

    in_list = (asked_list[:, None] == jnp.arange(lists_here, dtype=jnp.int32)[None, :]).astype(
        jnp.bfloat16
    )
    place = jnp.arange(slots, dtype=jnp.int32)
    earlier = (place[None, :] < place[:, None]).astype(jnp.bfloat16)
    before = jnp.dot(earlier, in_list, preferred_element_type=jnp.float32)
    order = jnp.sum(before * in_list.astype(jnp.float32), axis=1).astype(jnp.int32)
    valid = asked_list >= 0
    spot = jnp.where(valid, asked_list * list_capacity + order, -1)
    hit = spot[:, None] == jnp.arange(lists_here * list_capacity, dtype=jnp.int32)[None, :]
    grouped_row = jnp.sum(jnp.where(hit, row_of[:, None], 0), axis=0)
    grouped = select_rows(everyone, grouped_row, query_count, width)
    blocks = score(grouped, lists, spot, device_count)
    answer_rows = capacity * list_size // LANES
    got = exchange(blocks).astype(jnp.float32)
    powers = got[:, answer_rows:].reshape(device_count, -1)[:, :capacity].reshape(slots, 1)
    returned = (
        got[:, :answer_rows]
        .reshape(device_count, list_size // LANES, capacity, LANES)
        .transpose(0, 2, 1, 3)
        .reshape(slots, list_size)
    )
    returned = (returned + 32768.0) * (jnp.exp2(powers) / 65535.0)
    return returned[position].reshape(query_count, probe_count, list_size)


def solution(mesh):
    placed = (
        P(AXES, None),
        P(),
        P(AXES, None, None),
        P(AXES, None),
        P(),
    )
    return jax.shard_map(
        body, mesh=mesh, in_specs=placed, out_specs=P(AXES, None, None), check_vma=False
    )
```

```python
import jax
import jax.numpy as jnp
from jax import lax
from jax.experimental import pallas as pl
from jax.experimental.pallas import tpu as pltpu
from jax.sharding import PartitionSpec as P

AXES = ("grp", "own")
LANES = 128
LOG2E = 1.4426950408889634
LN2 = 0.6931471805599453


def gather_kernel(mine_ref, all_ref, send_sem, recv_sem):
    grp, own = lax.axis_index("grp"), lax.axis_index("own")
    z, x, y, c = grp // 2, grp % 2, own // 2, own % 2

    def device(zz, xx, yy, cc):
        return (zz * 2 + xx, yy * 2 + cc)

    def number(zz, xx, yy, cc):
        return (zz * 2 + xx) * 4 + yy * 2 + cc

    zs = [z] + [lax.rem(z + k, 4) for k in (1, 2, 3)]
    over_z = [device(zz, x, y, c) for zz in zs[1:]]
    over_x, over_y = device(z, 1 - x, y, c), device(z, x, 1 - y, c)
    sibling = device(z, x, y, 1 - c)
    barrier = pltpu.get_barrier_semaphore()
    for peer in over_z + [over_x, over_y, sibling]:
        pl.semaphore_signal(barrier, inc=1, device_id=peer, device_id_type=pl.DeviceIdType.MESH)
    pl.semaphore_wait(barrier, 6)

    sent = []
    rows = mine_ref.shape[0]
    middle = rows // 32 * 16
    halves = ((0, middle), (middle, rows - middle))

    def cut(ref, half):
        return ref.at[pl.ds(*halves[half])]

    def describe(src, block, half, peer, slot):
        return pltpu.make_async_remote_copy(
            src_ref=src,
            dst_ref=cut(all_ref.at[block], half),
            send_sem=send_sem.at[slot],
            recv_sem=recv_sem.at[half, block],
            device_id=peer,
            device_id_type=pl.DeviceIdType.MESH,
        )

    def send(src, block, half, peer):
        copy = describe(src, block, half, peer, len(sent))
        copy.start()
        sent.append(copy)

    def arrived(block, half):
        ref = cut(all_ref.at[block], half)
        describe(ref, block, half, sibling, 0).wait_recv()
        return ref

    me = number(z, x, y, c)
    for half in (0, 1):
        for peer in over_z + [over_x, over_y, sibling]:
            send(cut(mine_ref, half), me, half, peer)
    all_ref[me] = mine_ref[...]
    for k in (0, 1, 3, 2):
        for half in (0, 1):
            if k:
                block = number(zs[k], x, y, c)
                ref = arrived(block, half)
                for peer in (over_x, over_y, sibling):
                    send(ref, block, half, peer)
            block = number(zs[k], 1 - x, y, c)
            ref = arrived(block, half)
            if k % 2 == 1:
                send(ref, block, half, over_y)
            send(ref, block, half, sibling)
            block = number(zs[k], x, 1 - y, c)
            ref = arrived(block, half)
            if k % 2 == 0:
                send(ref, block, half, over_x)
            send(ref, block, half, sibling)
    for k in (0, 1, 3, 2):
        for half in (0, 1):
            block = number(zs[k], 1 - x, 1 - y, c)
            send(arrived(block, half), block, half, sibling)
    for k in (0, 1, 3, 2):
        for half in (0, 1):
            for xx in (x, 1 - x):
                for yy in (y, 1 - y):
                    arrived(number(zs[k], xx, yy, 1 - c), half)
    for copy in sent:
        copy.wait_send()


def gather_all(block):
    group_count, owner_count = lax.axis_size("grp"), lax.axis_size("own")
    if (group_count, owner_count) != (8, 4):
        return lax.all_gather(block, AXES, tiled=False)
    device_count = group_count * owner_count
    return pl.pallas_call(
        gather_kernel,
        out_shape=jax.ShapeDtypeStruct((device_count,) + block.shape, block.dtype),
        in_specs=[pl.BlockSpec(memory_space=pltpu.VMEM)],
        out_specs=pl.BlockSpec(memory_space=pltpu.VMEM),
        scratch_shapes=[
            pltpu.SemaphoreType.DMA((2 * device_count,)),
            pltpu.SemaphoreType.DMA((2, device_count)),
        ],
        compiler_params=pltpu.CompilerParams(
            collective_id=0, has_side_effects=True, vmem_limit_bytes=16 * 2**20
        ),
    )(block)


def select_kernel(queries, width, row_ref, all_ref, out_ref):
    devices = all_ref.shape[0]
    count = out_ref.shape[0]
    numbers = lax.broadcasted_iota(jnp.int32, (count, devices * queries), 1)
    pick = (numbers == row_ref[...]).astype(jnp.float32).astype(jnp.bfloat16)
    for j in range(width // LANES):
        part = all_ref[:, j * queries : (j + 1) * queries, :].reshape(devices * queries, LANES)
        out_ref[:, j * LANES : (j + 1) * LANES] = jnp.dot(
            pick, part, preferred_element_type=jnp.float32
        ).astype(jnp.bfloat16)


def select_rows(everyone, row_of, queries, width):
    slots = row_of.shape[0]
    block = min(256, slots)
    return pl.pallas_call(
        lambda *refs: select_kernel(queries, width, *refs),
        grid=(slots // block,),
        out_shape=jax.ShapeDtypeStruct((slots, width), jnp.bfloat16),
        in_specs=[
            pl.BlockSpec((block, 1), lambda i: (i, 0)),
            pl.BlockSpec(memory_space=pltpu.VMEM),
        ],
        out_specs=pl.BlockSpec((block, width), lambda i: (i, 0)),
        compiler_params=pltpu.CompilerParams(
            vmem_limit_bytes=48 * 2**20
        ),
    )(row_of[:, None], everyone)


def score_kernel(blocks, rows_ref, lists_ref, spot_ref, out_ref, held):
    step = pl.program_id(0)
    count, list_size, width = lists_ref.shape
    capacity = rows_ref.shape[0] // count
    for n in range(count):
        rows = rows_ref[n * capacity : (n + 1) * capacity, :]
        dots = lax.dot_general(
            rows, lists_ref[n], (((1,), (1,)), ((), ())), preferred_element_type=jnp.float32
        )
        rows_f = rows.astype(jnp.float32)
        row_norm = jnp.sum(rows_f * rows_f, axis=1, keepdims=True)
        partial = None
        for j in range(width // LANES):
            part = lists_ref[n, :, j * LANES : (j + 1) * LANES].astype(jnp.float32)
            partial = part * part if partial is None else partial + part * part
        vec_norm = jnp.sum(partial.T, axis=0, keepdims=True)
        distance = jnp.maximum((row_norm + vec_norm - 2.0 * dots) / width, 0.0)
        largest = jnp.maximum(jnp.max(distance, axis=1, keepdims=True), 1e-30)
        power = jnp.clip(jnp.ceil(jnp.log(largest) * LOG2E + 1e-3), -100.0, 120.0)
        code = jnp.clip(jnp.round(distance * (65535.0 * jnp.exp(power * -LN2))), 0.0, 65535.0)
        high = jnp.floor(code * (1.0 / 256.0))
        low = code - high * 256.0
        place = pl.ds(pl.multiple_of((step * count + n) * capacity, 16), capacity)
        held[place, :list_size] = high.astype(jnp.bfloat16)
        held[place, list_size : 2 * list_size] = low.astype(jnp.bfloat16)
        held[place, 2 * list_size :] = jnp.broadcast_to(power, (capacity, LANES)).astype(
            jnp.bfloat16
        )

    @pl.when(step == pl.num_programs(0) - 1)
    def _():
        slots = held.shape[0]
        each = slots // blocks
        numbers = lax.broadcasted_iota(jnp.int32, (slots, slots), 1)
        pick = (numbers == spot_ref[...]).astype(jnp.float32).astype(jnp.bfloat16)
        got = jnp.dot(pick, held[...], preferred_element_type=jnp.float32)
        code = got[:, :list_size] * 256.0 + got[:, list_size : 2 * list_size] - 32768.0
        parts = [
            code[:, h * LANES : (h + 1) * LANES].reshape(blocks, each, LANES)
            for h in range(list_size // LANES)
        ]
        powers = got[:, 2 * list_size :].reshape(blocks, each, LANES)
        slot = lax.broadcasted_iota(jnp.int32, powers.shape, 1)
        lane = lax.broadcasted_iota(jnp.int32, powers.shape, 2)
        powers = jnp.sum(jnp.where(slot == lane, powers, 0.0), axis=1, keepdims=True)
        parts.append(jnp.broadcast_to(powers, (blocks, 16, LANES)))
        whole = jnp.concatenate(parts, axis=1)
        out_ref[...] = whole.astype(jnp.int32).astype(jnp.int16)


def score(grouped, lists, spot, blocks):
    list_count, list_size, width = lists.shape
    slots = grouped.shape[0]
    count = 4
    out_rows = (slots // blocks) * list_size // LANES + 16
    return pl.pallas_call(
        lambda *refs: score_kernel(blocks, *refs),
        grid=(list_count // count,),
        out_shape=jax.ShapeDtypeStruct((blocks, out_rows, LANES), jnp.int16),
        in_specs=[
            pl.BlockSpec((slots // list_count * count, width), lambda i: (i, 0)),
            pl.BlockSpec((count, list_size, width), lambda i: (i, 0, 0)),
            pl.BlockSpec((slots, 1), lambda i: (0, 0)),
        ],
        out_specs=pl.BlockSpec((blocks, out_rows, LANES), lambda i: (0, 0, 0)),
        scratch_shapes=[pltpu.VMEM((slots, 2 * list_size + LANES), jnp.bfloat16)],
        compiler_params=pltpu.CompilerParams(vmem_limit_bytes=40 * 2**20),
    )(grouped, lists, spot[:, None])


def exchange_kernel(device_count, owner_count, out_ref, in_ref, send_sem, recv_sem):
    me = lax.axis_index("grp") * owner_count + lax.axis_index("own")

    def at(k):
        other = lax.rem(me + k, device_count)
        return other, (other // owner_count, lax.rem(other, owner_count))

    barrier = pltpu.get_barrier_semaphore()

    @pl.loop(1, device_count)
    def _(k):
        pl.semaphore_signal(
            barrier, inc=1, device_id=at(k)[1], device_id_type=pl.DeviceIdType.MESH
        )

    pl.semaphore_wait(barrier, device_count - 1)

    def describe(k, block):
        other, where = at(k)
        return pltpu.make_async_remote_copy(
            src_ref=out_ref.at[other],
            dst_ref=in_ref.at[block],
            send_sem=send_sem.at[k],
            recv_sem=recv_sem.at[block],
            device_id=where,
            device_id_type=pl.DeviceIdType.MESH,
        )

    @pl.loop(1, device_count)
    def _(k):
        describe(k, me).start()

    in_ref[me] = out_ref[me]

    @pl.loop(1, device_count)
    def _(k):
        describe(k, at(k)[0]).wait_recv()

    @pl.loop(1, device_count)
    def _(k):
        describe(k, me).wait_send()


def exchange(blocks):
    owner_count = lax.axis_size("own")
    device_count = blocks.shape[0]
    return pl.pallas_call(
        lambda *refs: exchange_kernel(device_count, owner_count, *refs),
        out_shape=jax.ShapeDtypeStruct(blocks.shape, blocks.dtype),
        in_specs=[pl.BlockSpec(memory_space=pltpu.VMEM)],
        out_specs=pl.BlockSpec(memory_space=pltpu.VMEM),
        scratch_shapes=[
            pltpu.SemaphoreType.DMA((device_count,)),
            pltpu.SemaphoreType.DMA((device_count,)),
        ],
        compiler_params=pltpu.CompilerParams(
            collective_id=1, has_side_effects=True, vmem_limit_bytes=16 * 2**20
        ),
    )(blocks)


def body(queries, projection, lists, probes, owner_map):
    query_count, width = queries.shape
    probe_count = probes.shape[1]
    lists_here, list_size = lists.shape[0], lists.shape[1]
    device_count = lax.axis_size("grp") * lax.axis_size("own")
    pairs = query_count * probe_count
    capacity = 2 * pairs // device_count
    list_capacity = device_count * capacity // lists_here
    slots = device_count * capacity
    me = lax.axis_index(AXES)

    projected = jnp.dot(queries, projection, preferred_element_type=jnp.float32).astype(
        jnp.bfloat16
    )
    stored = jnp.take(owner_map, probes.reshape(-1))
    target = stored // lists_here
    local = stored % lists_here
    to_target = (target[:, None] == jnp.arange(device_count, dtype=jnp.int32)[None, :]).astype(
        jnp.bfloat16
    )
    step = jnp.arange(pairs, dtype=jnp.int32)
    earlier = (step[None, :] < step[:, None]).astype(jnp.bfloat16)
    before = jnp.dot(earlier, to_target, preferred_element_type=jnp.float32)
    rank = jnp.sum(before * to_target.astype(jnp.float32), axis=1).astype(jnp.int32)
    position = target * capacity + rank

    at_rank = (rank[:, None] == jnp.arange(capacity, dtype=jnp.int32)[None, :]).astype(jnp.bfloat16)
    query_of = step // probe_count
    what = jnp.stack([jnp.ones_like(step), query_of, local], axis=0).astype(jnp.bfloat16)
    weighted = to_target.T[None] * what[:, None, :]
    table = jnp.dot(
        weighted.reshape(3 * device_count, pairs), at_rank, preferred_element_type=jnp.float32
    ).reshape(3, device_count, capacity)
    table = jnp.where(table[:1] > 0.5, table[1:], -1.0).astype(jnp.bfloat16)
    columns = width // LANES
    extra = -(-(2 * slots) // (16 * LANES)) * 16
    table = jnp.pad(table.reshape(-1), (0, extra * LANES - 2 * slots)).reshape(extra, LANES)
    stacked = projected.reshape(query_count, columns, LANES).transpose(1, 0, 2)
    stacked = stacked.reshape(columns * query_count, LANES)

    everyone = gather_all(jnp.concatenate([stacked, table], axis=0))
    tables = everyone[:, columns * query_count :].reshape(device_count, -1)[:, : 2 * slots]
    tables = tables.reshape(device_count, 2, device_count, capacity)
    mine = lax.dynamic_index_in_dim(tables, me, axis=2, keepdims=False).astype(jnp.int32)
    asked_query = mine[:, 0].reshape(-1)
    asked_list = mine[:, 1].reshape(-1)
    row_of = (
        asked_query + query_count * (jnp.arange(slots, dtype=jnp.int32) // capacity)
    )

    in_list = (asked_list[:, None] == jnp.arange(lists_here, dtype=jnp.int32)[None, :]).astype(
        jnp.bfloat16
    )
    place = jnp.arange(slots, dtype=jnp.int32)
    earlier = (place[None, :] < place[:, None]).astype(jnp.bfloat16)
    before = jnp.dot(earlier, in_list, preferred_element_type=jnp.float32)
    order = jnp.sum(before * in_list.astype(jnp.float32), axis=1).astype(jnp.int32)
    valid = asked_list >= 0
    spot = jnp.where(valid, asked_list * list_capacity + order, -1)
    hit = spot[:, None] == jnp.arange(lists_here * list_capacity, dtype=jnp.int32)[None, :]
    grouped_row = jnp.sum(jnp.where(hit, row_of[:, None], 0), axis=0)
    grouped = select_rows(everyone, grouped_row, query_count, width)
    blocks = score(grouped, lists, spot, device_count)
    answer_rows = capacity * list_size // LANES
    got = exchange(blocks).astype(jnp.float32)
    powers = got[:, answer_rows:].reshape(device_count, -1)[:, :capacity].reshape(slots, 1)
    returned = (
        got[:, :answer_rows]
        .reshape(device_count, list_size // LANES, capacity, LANES)
        .transpose(0, 2, 1, 3)
        .reshape(slots, list_size)
    )
    returned = (returned + 32768.0) * (jnp.exp2(powers) / 65535.0)
    return returned[position].reshape(query_count, probe_count, list_size)


def solution(mesh):
    placed = (
        P(AXES, None),
        P(),
        P(AXES, None, None),
        P(AXES, None),
        P(),
    )
    return jax.shard_map(
        body, mesh=mesh, in_specs=placed, out_specs=P(AXES, None, None), check_vma=False
    )
```
